32 devices in a mesh: dp: 2 (over x), mp: 16 (over z, y, core).
Axes of the slice: x: 2, y: 2, z: 4, core: 2. Of those that a mesh axis runs over, the one named last changes fastest.
Arguments:
- tokens: bfloat16 [256, 8192], P('dp', 'mp'), may hold values from -6 to 6
- gate_weight: bfloat16 [8192, 14336], P('mp', 'dp'), may hold values from -0.0625 to 0.0625
- up_weight: bfloat16 [8192, 14336], P('mp', 'dp'), may hold values from -0.0625 to 0.0625
- down_weight: bfloat16 [14336, 8192], P('dp', 'mp'), may hold values from -0.046875 to 0.046875
- factor_self: bfloat16 [5, 8192, 256], P(None, 'mp'), may hold values from -0.25 to 0.25
- factor_cross: bfloat16 [5, 8192, 256], P(None, 'mp'), may hold values from -0.25 to 0.25
- cotangent: bfloat16 [256, 8192], P('dp', 'mp'), may hold values from -1.1953125 to 1.1953125
Outputs:
- mixed_out: bfloat16 [256, 8192], P('dp', 'mp')
- input_grad: bfloat16 [256, 8192], P('dp', 'mp')
- self_grad: float32 [5, 8192, 256], P(None, 'mp')
- cross_grad: float32 [5, 8192, 256], P(None, 'mp')
The draws below stay inside these ranges and needn't reach their ends.
All inputs are finite; a program needn't handle non-finite values.
Results may differ from the reference program's by a relative error of at most 0.04.
Values may be sent and summed in bfloat16 or wider, within the bound.
A program may use at most 128 MiB of HBM per device.

```python
import jax
import jax.numpy as jnp
from jax import lax

D = 8192
FF = 14336
BLOCK = 256
SECTIONS = 5
TOKENS = 256
N_MP = 16


def level_of(key, extent, pieces, least, high):
    def one(axis_at, blocks):
        draws = jax.random.uniform(jax.random.fold_in(jax.random.fold_in(key, 6), axis_at), (blocks,), jnp.float32, least / len(pieces), high / len(pieces))
        return jnp.repeat(jnp.exp(draws), extent[axis_at] // blocks).reshape((-1,) + (1,) * (len(extent) - axis_at - 1))

    factor_of = one(*pieces[0])
    for cut in pieces[1:]:
        factor_of = factor_of * one(*cut)
    return factor_of


def centred(key, extent, deviation, bound, shards=(), kind=jnp.bfloat16):
    entries = deviation * jax.random.normal(key, extent, jnp.float32)
    if shards:
        entries = entries * level_of(key, extent, shards, -0.22, 0.18)
    return jnp.clip(entries, -bound, bound).astype(kind)


def setup_inputs(seed: int = 0) -> dict:
    key_of = jax.random.split(jax.random.key(seed), 8)
    tokens = centred(key_of[0], (TOKENS, D), 1.0, 6.0, ((0, 2), (1, 16)))
    gate_weight = centred(key_of[1], (D, FF), D ** -0.5, 0.0625, ((0, 16), (1, 2)))
    up_weight = centred(key_of[2], (D, FF), D ** -0.5, 0.0625, ((0, 16), (1, 2)))
    down_weight = centred(key_of[3], (FF, D), FF ** -0.5, 0.046875, ((0, 2), (1, 16)))
    factor_self = centred(key_of[4], (SECTIONS, D, BLOCK), (2 * BLOCK) ** -0.5, 0.25, ((1, 16),))
    factor_cross = centred(key_of[5], (SECTIONS, D, BLOCK), (2 * BLOCK) ** -0.5, 0.25, ((1, 16),))
    cotangent = centred(key_of[6], (TOKENS, D), 0.2, 1.1953125, ((0, 2), (1, 16)))
    return {"tokens": tokens, "gate_weight": gate_weight, "up_weight": up_weight, "down_weight": down_weight, "factor_self": factor_self, "factor_cross": factor_cross, "cotangent": cotangent}


def partner_blocks(blocks, degree):
    tok_rows, amount, breadth = blocks.shape
    distance = 2 ** degree
    folded = blocks.reshape(tok_rows, amount // (2 * distance), 2, distance, breadth)
    return jnp.flip(folded, 2).reshape(tok_rows, amount, breadth)


def grouped(left_side, right_side):
    group_rows = D // N_MP

    def add_group(running, group_idx):
        start_at = (group_idx * group_rows).astype(jnp.int32)
        left_part = lax.dynamic_slice_in_dim(left_side, start_at, group_rows, 1)
        right_part = lax.dynamic_slice_in_dim(right_side, start_at, group_rows, 0)
        portion = jnp.dot(left_part, right_part, preferred_element_type=jnp.float32)
        portion = lax.optimization_barrier(portion.astype(jnp.bfloat16)).astype(jnp.float32)
        return running + portion, None

    initial = jnp.zeros((left_side.shape[0], right_side.shape[1]), jnp.float32)
    running, _ = lax.scan(add_group, initial, jnp.arange(N_MP, dtype=jnp.int32))
    return running


def reference(tokens, gate_weight, up_weight, down_weight, factor_self, factor_cross, cotangent):
    amount = D // BLOCK
    highest = lax.Precision.HIGHEST
    current = tokens.reshape(TOKENS, amount, BLOCK)
    inputs = []
    partners = []
    for degree in range(SECTIONS):
        self_mat = factor_self[degree].reshape(amount, BLOCK, BLOCK).astype(jnp.float32)
        cross_mat = factor_cross[degree].reshape(amount, BLOCK, BLOCK).astype(jnp.float32)
        partner = partner_blocks(current, degree)
        inputs.append(current)
        partners.append(partner)
        result = jnp.einsum('tkb,kbc->tkc', current.astype(jnp.float32), self_mat, precision=highest)
        result = result + jnp.einsum('tkb,kbc->tkc', partner.astype(jnp.float32), cross_mat, precision=highest)
        current = result.astype(jnp.bfloat16)
    rotated = current.reshape(TOKENS, D)
    gate_sum = grouped(rotated, gate_weight)
    up_sum = grouped(rotated, up_weight)
    hidden = (jax.nn.silu(gate_sum) * up_sum).astype(jnp.bfloat16)
    mixed_out = jnp.dot(hidden, down_weight, preferred_element_type=jnp.float32).astype(jnp.bfloat16)
    hidden_grad = grouped(cotangent, down_weight.T)
    logistic = jax.nn.sigmoid(gate_sum)
    gate_grad = (hidden_grad * up_sum * logistic * (1.0 + gate_sum * (1.0 - logistic))).astype(jnp.bfloat16)
    up_grad = (hidden_grad * gate_sum * logistic).astype(jnp.bfloat16)
    rotated_grad = jnp.dot(gate_grad, gate_weight.T, preferred_element_type=jnp.float32)
    rotated_grad = rotated_grad + jnp.dot(up_grad, up_weight.T, preferred_element_type=jnp.float32)
    gradient = rotated_grad.astype(jnp.bfloat16).reshape(TOKENS, amount, BLOCK)
    self_list = [None] * SECTIONS
    cross_list = [None] * SECTIONS
    for degree in reversed(range(SECTIONS)):
        self_mat = factor_self[degree].reshape(amount, BLOCK, BLOCK).astype(jnp.float32)
        cross_mat = factor_cross[degree].reshape(amount, BLOCK, BLOCK).astype(jnp.float32)
        grad_f = gradient.astype(jnp.float32)
        self_list[degree] = jnp.einsum('tkb,tkc->kbc', inputs[degree].astype(jnp.float32), grad_f, precision=highest).reshape(D, BLOCK)
        cross_list[degree] = jnp.einsum('tkb,tkc->kbc', partners[degree].astype(jnp.float32), grad_f, precision=highest).reshape(D, BLOCK)
        direct = jnp.einsum('tkc,kbc->tkb', grad_f, self_mat, precision=highest)
        carried = jnp.einsum('tkc,kbc->tkb', grad_f, cross_mat, precision=highest)
        gradient = (direct + partner_blocks(carried, degree)).astype(jnp.bfloat16)
    input_grad = gradient.reshape(TOKENS, D)
    return mixed_out, input_grad, jnp.stack(self_list), jnp.stack(cross_list)
```

```python
import jax
import jax.numpy as jnp
from jax import lax
from jax.sharding import PartitionSpec as P

BLOCK = 256
SECTIONS = 5


def swapped(block, axis, stride):
    count = lax.axis_size(axis)
    route = []
    for low in range(count):
        high = low | 1 << stride
        if high != low and high < count:
            route += [(low, high), (high, low)]
    return lax.ppermute(block, axis, route)


def gather_dp(block):
    if lax.axis_size("dp") == 2:
        return jnp.concatenate([block, swapped(block, "dp", 0)], axis=0)
    return lax.all_gather(block, "dp", axis=0, tiled=True)


def scatter_dp(total):
    if lax.axis_size("dp") == 2:
        rows = total.shape[0] // 2
        return (
            total[:rows] + swapped(total[rows:].astype(jnp.bfloat16), "dp", 0).astype(jnp.float32)
        ).astype(jnp.bfloat16)
    return lax.psum_scatter(total.astype(jnp.bfloat16), "dp", scatter_dimension=0, tiled=True)


def local_partner(blocks, degree):
    tok_rows, amount, breadth = blocks.shape
    distance = 2**degree
    folded = blocks.reshape(tok_rows, amount // (2 * distance), 2, distance, breadth)
    return jnp.flip(folded, 2).reshape(tok_rows, amount, breadth)


def contract_last(left_side, right_side):
    return lax.dot_general(
        left_side, right_side, (((1,), (1,)), ((), ())), preferred_element_type=jnp.float32
    )


def reduce_mp(partial):
    return lax.psum_scatter(
        partial.astype(jnp.bfloat16), "mp", scatter_dimension=0, tiled=True
    ).astype(jnp.float32)


def gather_mp(share):
    return lax.all_gather(share, "mp", axis=0, tiled=True)


def per_device(tokens, gate_weight, up_weight, down_weight, factor_self, factor_cross, cotangent):
    tok_rows, local_width = tokens.shape
    per_dev = local_width // BLOCK
    local_bits = per_dev.bit_length() - 1
    hidden_grad = reduce_mp(contract_last(gather_dp(cotangent), down_weight))
    current = tokens.reshape(tok_rows, per_dev, BLOCK)
    kept = []
    for degree in range(SECTIONS):
        self_mat = factor_self[degree].reshape(per_dev, BLOCK, BLOCK)
        cross_mat = factor_cross[degree].reshape(per_dev, BLOCK, BLOCK)
        if degree < local_bits:
            partner = local_partner(current, degree)
            kept += [current.reshape(tok_rows, local_width)]
        else:
            partner = swapped(current, "mp", degree - local_bits)
            kept += [current.reshape(tok_rows, local_width), partner.reshape(tok_rows, local_width)]
        result = jnp.einsum("tkb,kbc->tkc", current, self_mat, preferred_element_type=jnp.float32)
        result = result + jnp.einsum(
            "tkb,kbc->tkc", partner, cross_mat, preferred_element_type=jnp.float32
        )
        current = result.astype(jnp.bfloat16)
    rotated = current.reshape(tok_rows, local_width)
    segment = gather_dp(rotated)
    kept = gather_dp(jnp.concatenate(kept, axis=1))
    gate_sum = reduce_mp(jnp.dot(segment, gate_weight, preferred_element_type=jnp.float32))
    up_sum = reduce_mp(jnp.dot(segment, up_weight, preferred_element_type=jnp.float32))
    logistic = jax.nn.sigmoid(gate_sum)
    gate_grad = (hidden_grad * up_sum * logistic * (1.0 + gate_sum * (1.0 - logistic))).astype(
        jnp.bfloat16
    )
    up_grad = (hidden_grad * gate_sum * logistic).astype(jnp.bfloat16)
    hidden = (jax.nn.silu(gate_sum) * up_sum).astype(jnp.bfloat16)
    rot_terms = contract_last(gather_mp(gate_grad), gate_weight) + contract_last(
        gather_mp(up_grad), up_weight
    )
    gradient = scatter_dp(rot_terms)
    partial_value = jnp.dot(gather_mp(hidden), down_weight, preferred_element_type=jnp.float32)
    mixed_out = scatter_dp(partial_value)

    all_rows = kept.shape[0]
    kept = kept.reshape(all_rows, -1, per_dev, BLOCK)
    place = kept.shape[1]
    gradient = gradient.reshape(tok_rows, per_dev, BLOCK)
    self_list = [None] * SECTIONS
    cross_list = [None] * SECTIONS
    for degree in reversed(range(SECTIONS)):
        self_mat = factor_self[degree].reshape(per_dev, BLOCK, BLOCK)
        cross_mat = factor_cross[degree].reshape(per_dev, BLOCK, BLOCK)
        gathered = gather_dp(gradient)
        if degree < local_bits:
            place -= 1
            ours = kept[:, place]
            theirs = local_partner(ours, degree)
        else:
            place -= 2
            ours, theirs = kept[:, place], kept[:, place + 1]
        self_list[degree] = jnp.einsum(
            "tkb,tkc->kbc", ours, gathered, preferred_element_type=jnp.float32
        ).reshape(per_dev * BLOCK, BLOCK)
        cross_list[degree] = jnp.einsum(
            "tkb,tkc->kbc", theirs, gathered, preferred_element_type=jnp.float32
        ).reshape(per_dev * BLOCK, BLOCK)
        direct = jnp.einsum("tkc,kbc->tkb", gradient, self_mat, preferred_element_type=jnp.float32)
        carried = jnp.einsum(
            "tkc,kbc->tkb", gradient, cross_mat, preferred_element_type=jnp.float32
        )
        if degree < local_bits:
            returned = local_partner(carried, degree)
        else:
            returned = swapped(carried.astype(jnp.bfloat16), "mp", degree - local_bits).astype(
                carried.dtype
            )
        gradient = (direct + returned).astype(jnp.bfloat16)
    self_grad = jnp.stack(self_list)
    cross_grad = jnp.stack(cross_list)
    return (mixed_out, gradient.reshape(tok_rows, local_width), self_grad, cross_grad)


def solution(mesh):
    return jax.shard_map(
        per_device,
        mesh=mesh,
        in_specs=(
            P("dp", "mp"),
            P("mp", "dp"),
            P("mp", "dp"),
            P("dp", "mp"),
            P(None, "mp", None),
            P(None, "mp", None),
            P("dp", "mp"),
        ),
        out_specs=(P("dp", "mp"), P("dp", "mp"), P(None, "mp", None), P(None, "mp", None)),
        check_vma=False,
    )
```

```python
import functools

import jax
import jax.numpy as jnp
from jax import lax
from jax.experimental import pallas as pl
from jax.experimental.pallas import tpu as pltpu
from jax.sharding import PartitionSpec as P

BLOCK = 256
SECTIONS = 5


def swapped(block, axis, stride):
    count = lax.axis_size(axis)
    route = []
    for low in range(count):
        high = low | 1 << stride
        if high != low and high < count:
            route += [(low, high), (high, low)]
    return lax.ppermute(block, axis, route)


def gather_dp(block):
    if lax.axis_size("dp") == 2:
        return jnp.concatenate([block, swapped(block, "dp", 0)], axis=0)
    return lax.all_gather(block, "dp", axis=0, tiled=True)


def scatter_dp(total):
    if lax.axis_size("dp") == 2:
        rows = total.shape[0] // 2
        return (
            total[:rows] + swapped(total[rows:].astype(jnp.bfloat16), "dp", 0).astype(jnp.float32)
        ).astype(jnp.bfloat16)
    return lax.psum_scatter(total.astype(jnp.bfloat16), "dp", scatter_dimension=0, tiled=True)


def local_partner(blocks, degree):
    tok_rows, amount, breadth = blocks.shape
    distance = 2**degree
    folded = blocks.reshape(tok_rows, amount // (2 * distance), 2, distance, breadth)
    return jnp.flip(folded, 2).reshape(tok_rows, amount, breadth)


def contract_last(left_side, right_side):
    return lax.dot_general(
        left_side, right_side, (((1,), (1,)), ((), ())), preferred_element_type=jnp.float32
    )


def column_chunks(width):
    for count in (4, 2):
        if width % (count * 128) == 0:
            return count, width // count
    return 1, width


def halves_of(me, stages, rows):
    bits, starts, start = [], [], 0
    for stage in range(stages):
        bit = lax.rem(lax.div(me, 1 << stage), 2)
        bits.append(bit)
        starts.append(start)
        start = start + bit * (rows >> (stage + 1))
    starts.append(start)
    return bits, starts


def greet(partners):
    barrier = pltpu.get_barrier_semaphore()
    for partner in partners:
        pl.semaphore_signal(
            barrier, inc=1, device_id={"mp": partner}, device_id_type=pl.DeviceIdType.MESH
        )
    pl.semaphore_wait(barrier, len(partners))


def reduce_kernel(stages, amount, turned, *refs):
    left_ref, weights, outs = refs[0], refs[1 : 1 + amount], refs[1 + amount : 1 + 2 * amount]
    weight_buf, part, *arrived, load_sem, send_sem, recv_sem = refs[1 + 2 * amount :]
    rows = left_ref.shape[0]
    width = outs[0].shape[1]
    per_array, span = column_chunks(width)
    chunks = [(array, piece) for array in range(amount) for piece in range(per_array)]
    me = lax.axis_index("mp")

    loads = []
    for at, (array, piece) in enumerate(chunks):
        cut = pl.ds(piece * span, span)
        source = weights[array].at[cut, :] if turned else weights[array].at[:, cut]
        loads.append(pltpu.make_async_copy(source, weight_buf.at[at], load_sem.at[at]))
        loads[-1].start()

    bits, _ = halves_of(me, stages, rows)
    partners = [me + (1 - 2 * bits[stage]) * (1 << stage) for stage in range(stages)]
    greet(partners)

    copies = {}

    def current(stage, at):
        return part.at[at] if stage == 0 else arrived[stage - 1].at[at]

    def send(stage, at):
        half = rows >> (stage + 1)
        first = pl.multiple_of((1 - bits[stage]) * half, half)
        copies[stage, at] = pltpu.make_async_remote_copy(
            src_ref=current(stage, at).at[pl.ds(first, half)],
            dst_ref=arrived[stage].at[at],
            send_sem=send_sem.at[stage, at],
            recv_sem=recv_sem.at[stage, at],
            device_id={"mp": partners[stage]},
            device_id_type=pl.DeviceIdType.MESH,
        )
        copies[stage, at].start()

    tile = 256 if span % 256 == 0 else 128 if span % 128 == 0 else span

    def multiply(at):
        loads[at].wait()

        def one(step, _):
            cut = pl.ds(pl.multiple_of(step * tile, tile), tile)
            if turned:
                product = contract_last(left_ref[...], weight_buf[at, cut, :])
            else:
                product = jnp.dot(
                    left_ref[...], weight_buf[at, :, cut], preferred_element_type=jnp.float32
                )
            part[at, :, cut] = product.astype(jnp.bfloat16)
            return 0

        lax.fori_loop(0, span // tile, one, 0)

    def receive(stage, at):
        copies[stage, at].wait_recv()
        half = rows >> (stage + 1)
        step_rows = min(half, 16)
        held = current(stage, at)
        first = bits[stage] * half
        array, piece = chunks[at]

        def one(step, _):
            here = pl.ds(pl.multiple_of(step * step_rows, step_rows), step_rows)
            there = pl.ds(pl.multiple_of(first + step * step_rows, step_rows), step_rows)
            total = arrived[stage][at, here, :].astype(jnp.float32) + held[there, :].astype(
                jnp.float32
            )
            if stage == stages - 1:
                outs[array][here, pl.ds(piece * span, span)] = total
            else:
                arrived[stage][at, here, :] = total.astype(jnp.bfloat16)
            return 0

        lax.fori_loop(0, half // step_rows, one, 0)
        if stage < stages - 1:
            send(stage + 1, at)

    for turn in range(len(chunks) + stages):
        if turn < len(chunks):
            multiply(turn)
            send(0, turn)
        for stage in range(stages):
            at = turn - 1 - stage
            if 0 <= at < len(chunks):
                receive(stage, at)
    for copy in copies.values():
        copy.wait_send()


def reduce_mp(left, weights, turned, identity):
    count = lax.axis_size("mp")
    stages = count.bit_length() - 1
    rows, depth = left.shape
    width = weights[0].shape[0 if turned else 1]
    amount = len(weights)
    per_array, span = column_chunks(width)
    chunks = amount * per_array
    return pl.pallas_call(
        functools.partial(reduce_kernel, stages, amount, turned),
        out_shape=[jax.ShapeDtypeStruct((rows // count, width), jnp.float32)] * amount,
        in_specs=[pl.BlockSpec(memory_space=pltpu.VMEM)]
        + [pl.BlockSpec(memory_space=pl.ANY)] * amount,
        out_specs=[pl.BlockSpec(memory_space=pltpu.VMEM)] * amount,
        scratch_shapes=[
            pltpu.VMEM((chunks, span, depth) if turned else (chunks, depth, span), jnp.bfloat16),
            pltpu.VMEM((chunks, rows, span), jnp.bfloat16),
        ]
        + [
            pltpu.VMEM((chunks, rows >> (stage + 1), span), jnp.bfloat16)
            for stage in range(stages)
        ]
        + [
            pltpu.SemaphoreType.DMA((chunks,)),
            pltpu.SemaphoreType.DMA((stages, chunks)),
            pltpu.SemaphoreType.DMA((stages, chunks)),
        ],
        compiler_params=pltpu.CompilerParams(
            collective_id=identity, has_side_effects=True, vmem_limit_bytes=48 << 20
        ),
        cost_estimate=pl.CostEstimate(
            flops=2 * rows * depth * width * amount,
            bytes_accessed=amount * width * (depth + 20 * rows) * 2,
            transcendentals=0,
        ),
    )(left, *weights)


def gather_kernel(stages, amount, *refs):
    shares, outs = refs[:amount], refs[amount : 2 * amount]
    send_sem, recv_sem = refs[2 * amount :]
    rows, width = outs[0].shape
    per_array, span = column_chunks(width)
    chunks = [(array, piece) for array in range(amount) for piece in range(per_array)]
    me = lax.axis_index("mp")
    bits, starts = halves_of(me, stages, rows)
    partners = [me + (1 - 2 * bits[stage]) * (1 << stage) for stage in range(stages)]
    least = rows >> stages
    own = pl.ds(pl.multiple_of(starts[stages], least), least)
    for array in range(amount):
        outs[array][own, :] = shares[array][...]
    greet(partners)

    copies = {}

    def send(stage, at):
        array, piece = chunks[at]
        size = rows >> (stage + 1)
        region = outs[array].at[
            pl.ds(pl.multiple_of(starts[stage + 1], size), size), pl.ds(piece * span, span)
        ]
        copies[stage, at] = pltpu.make_async_remote_copy(
            src_ref=region,
            dst_ref=region,
            send_sem=send_sem.at[stage, at],
            recv_sem=recv_sem.at[stage, at],
            device_id={"mp": partners[stage]},
            device_id_type=pl.DeviceIdType.MESH,
        )
        copies[stage, at].start()

    for turn in range(len(chunks) + stages):
        if turn < len(chunks):
            send(stages - 1, turn)
        for step in range(stages):
            at = turn - 1 - step
            stage = stages - 1 - step
            if 0 <= at < len(chunks):
                copies[stage, at].wait_recv()
                if stage > 0:
                    send(stage - 1, at)
    for copy in copies.values():
        copy.wait_send()


def gather_mp(shares, identity):
    count = lax.axis_size("mp")
    stages = count.bit_length() - 1
    rows, width = shares[0].shape
    amount = len(shares)
    chunks = amount * column_chunks(width)[0]
    return pl.pallas_call(
        functools.partial(gather_kernel, stages, amount),
        out_shape=[jax.ShapeDtypeStruct((rows * count, width), jnp.bfloat16)] * amount,
        in_specs=[pl.BlockSpec(memory_space=pltpu.VMEM)] * amount,
        out_specs=[pl.BlockSpec(memory_space=pltpu.VMEM)] * amount,
        scratch_shapes=[
            pltpu.SemaphoreType.DMA((stages, chunks)),
            pltpu.SemaphoreType.DMA((stages, chunks)),
        ],
        compiler_params=pltpu.CompilerParams(
            collective_id=identity, has_side_effects=True, vmem_limit_bytes=48 << 20
        ),
        cost_estimate=pl.CostEstimate(
            flops=0, bytes_accessed=amount * width * rows * count * 40, transcendentals=0
        ),
    )(*shares)


def per_device(tokens, gate_weight, up_weight, down_weight, factor_self, factor_cross, cotangent):
    tok_rows, local_width = tokens.shape
    per_dev = local_width // BLOCK
    local_bits = per_dev.bit_length() - 1
    (hidden_grad,) = reduce_mp(gather_dp(cotangent), [down_weight], True, 0)
    current = tokens.reshape(tok_rows, per_dev, BLOCK)
    kept = []
    for degree in range(SECTIONS):
        self_mat = factor_self[degree].reshape(per_dev, BLOCK, BLOCK)
        cross_mat = factor_cross[degree].reshape(per_dev, BLOCK, BLOCK)
        if degree < local_bits:
            partner = local_partner(current, degree)
            kept += [current.reshape(tok_rows, local_width)]
        else:
            partner = swapped(current, "mp", degree - local_bits)
            kept += [current.reshape(tok_rows, local_width), partner.reshape(tok_rows, local_width)]
        result = jnp.einsum("tkb,kbc->tkc", current, self_mat, preferred_element_type=jnp.float32)
        result = result + jnp.einsum(
            "tkb,kbc->tkc", partner, cross_mat, preferred_element_type=jnp.float32
        )
        current = result.astype(jnp.bfloat16)
    rotated = current.reshape(tok_rows, local_width)
    segment = gather_dp(rotated)
    kept = gather_dp(jnp.concatenate(kept, axis=1))
    gate_sum, up_sum = reduce_mp(segment, [gate_weight, up_weight], False, 1)
    logistic = jax.nn.sigmoid(gate_sum)
    gate_grad = (hidden_grad * up_sum * logistic * (1.0 + gate_sum * (1.0 - logistic))).astype(
        jnp.bfloat16
    )
    up_grad = (hidden_grad * gate_sum * logistic).astype(jnp.bfloat16)
    hidden = (jax.nn.silu(gate_sum) * up_sum).astype(jnp.bfloat16)
    gate_all, up_all = gather_mp([gate_grad, up_grad], 2)
    rot_terms = contract_last(gate_all, gate_weight) + contract_last(up_all, up_weight)
    gradient = scatter_dp(rot_terms)
    (hidden_all,) = gather_mp([hidden], 3)
    partial_value = jnp.dot(hidden_all, down_weight, preferred_element_type=jnp.float32)
    mixed_out = scatter_dp(partial_value)

    all_rows = kept.shape[0]
    kept = kept.reshape(all_rows, -1, per_dev, BLOCK)
    place = kept.shape[1]
    gradient = gradient.reshape(tok_rows, per_dev, BLOCK)
    self_list = [None] * SECTIONS
    cross_list = [None] * SECTIONS
    for degree in reversed(range(SECTIONS)):
        self_mat = factor_self[degree].reshape(per_dev, BLOCK, BLOCK)
        cross_mat = factor_cross[degree].reshape(per_dev, BLOCK, BLOCK)
        gathered = gather_dp(gradient)
        if degree < local_bits:
            place -= 1
            ours = kept[:, place]
            theirs = local_partner(ours, degree)
        else:
            place -= 2
            ours, theirs = kept[:, place], kept[:, place + 1]
        self_list[degree] = jnp.einsum(
            "tkb,tkc->kbc", ours, gathered, preferred_element_type=jnp.float32
        ).reshape(per_dev * BLOCK, BLOCK)
        cross_list[degree] = jnp.einsum(
            "tkb,tkc->kbc", theirs, gathered, preferred_element_type=jnp.float32
        ).reshape(per_dev * BLOCK, BLOCK)
        direct = jnp.einsum("tkc,kbc->tkb", gradient, self_mat, preferred_element_type=jnp.float32)
        carried = jnp.einsum(
            "tkc,kbc->tkb", gradient, cross_mat, preferred_element_type=jnp.float32
        )
        if degree < local_bits:
            returned = local_partner(carried, degree)
        else:
            returned = swapped(carried.astype(jnp.bfloat16), "mp", degree - local_bits).astype(
                carried.dtype
            )
        gradient = (direct + returned).astype(jnp.bfloat16)
    self_grad = jnp.stack(self_list)
    cross_grad = jnp.stack(cross_list)
    return (mixed_out, gradient.reshape(tok_rows, local_width), self_grad, cross_grad)


def solution(mesh):
    return jax.shard_map(
        per_device,
        mesh=mesh,
        in_specs=(
            P("dp", "mp"),
            P("mp", "dp"),
            P("mp", "dp"),
            P("dp", "mp"),
            P(None, "mp", None),
            P(None, "mp", None),
            P("dp", "mp"),
        ),
        out_specs=(P("dp", "mp"), P("dp", "mp"), P(None, "mp", None), P(None, "mp", None)),
        check_vma=False,
    )
```

```python
import functools

import jax
import jax.numpy as jnp
from jax import lax
from jax.experimental import pallas as pl
from jax.experimental.pallas import tpu as pltpu
from jax.sharding import PartitionSpec as P

BLOCK = 256
SECTIONS = 5


def swapped(block, axis, stride):
    count = lax.axis_size(axis)
    route = []
    for low in range(count):
        high = low | 1 << stride
        if high != low and high < count:
            route += [(low, high), (high, low)]
    return lax.ppermute(block, axis, route)


def gather_dp(block):
    if lax.axis_size("dp") == 2:
        return jnp.concatenate([block, swapped(block, "dp", 0)], axis=0)
    return lax.all_gather(block, "dp", axis=0, tiled=True)


def scatter_dp(total):
    if lax.axis_size("dp") == 2:
        rows = total.shape[0] // 2
        return (
            total[:rows] + swapped(total[rows:].astype(jnp.bfloat16), "dp", 0).astype(jnp.float32)
        ).astype(jnp.bfloat16)
    return lax.psum_scatter(total.astype(jnp.bfloat16), "dp", scatter_dimension=0, tiled=True)


def local_partner(blocks, degree):
    tok_rows, amount, breadth = blocks.shape
    distance = 2**degree
    folded = blocks.reshape(tok_rows, amount // (2 * distance), 2, distance, breadth)
    return jnp.flip(folded, 2).reshape(tok_rows, amount, breadth)


def contract_last(left_side, right_side):
    return lax.dot_general(
        left_side, right_side, (((1,), (1,)), ((), ())), preferred_element_type=jnp.float32
    )


def column_chunks(width):
    for count in (4, 2):
        if width % (count * 128) == 0:
            return count, width // count
    return 1, width


def halves_of(me, stages, rows):
    bits, starts, start = [], [], 0
    for stage in range(stages):
        bit = lax.rem(lax.div(me, 1 << stage), 2)
        bits.append(bit)
        starts.append(start)
        start = start + bit * (rows >> (stage + 1))
    starts.append(start)
    return bits, starts


def greet(partners):
    barrier = pltpu.get_barrier_semaphore()
    for partner in partners:
        pl.semaphore_signal(
            barrier, inc=1, device_id={"mp": partner}, device_id_type=pl.DeviceIdType.MESH
        )
    pl.semaphore_wait(barrier, len(partners))


def reduce_kernel(stages, plan, lefts_held, *refs):
    amount = len(plan)
    lefts, refs = refs[:lefts_held], refs[lefts_held:]
    weights, outs = refs[:amount], refs[amount : 2 * amount]
    turned_buf, plain_buf, part, *arrived, load_sem, send_sem, recv_sem = refs[2 * amount :]
    rows = lefts[0].shape[0]
    width = outs[0].shape[1]
    per_array, span = column_chunks(width)
    chunks = [(array, piece) for array in range(amount) for piece in range(per_array)]
    me = lax.axis_index("mp")

    loads, slots, used = [], [], [0, 0]
    for at, (array, piece) in enumerate(chunks):
        cut = pl.ds(piece * span, span)
        turned = plan[array][1]
        slots.append(used[turned])
        used[turned] += 1
        if turned:
            source, target = weights[array].at[cut, :], turned_buf.at[slots[at]]
        else:
            source, target = weights[array].at[:, cut], plain_buf.at[slots[at]]
        loads.append(pltpu.make_async_copy(source, target, load_sem.at[at]))
        loads[-1].start()

    bits, _ = halves_of(me, stages, rows)
    partners = [me + (1 - 2 * bits[stage]) * (1 << stage) for stage in range(stages)]
    greet(partners)

    copies = {}

    def current(stage, at):
        return part.at[at] if stage == 0 else arrived[stage - 1].at[at]

    def send(stage, at):
        half = rows >> (stage + 1)
        first = pl.multiple_of((1 - bits[stage]) * half, half)
        copies[stage, at] = pltpu.make_async_remote_copy(
            src_ref=current(stage, at).at[pl.ds(first, half)],
            dst_ref=arrived[stage].at[at],
            send_sem=send_sem.at[stage, at],
            recv_sem=recv_sem.at[stage, at],
            device_id={"mp": partners[stage]},
            device_id_type=pl.DeviceIdType.MESH,
        )
        copies[stage, at].start()

    tile = 256 if span % 256 == 0 else 128 if span % 128 == 0 else span

    def multiply(at):
        loads[at].wait()
        left, turned = plan[chunks[at][0]]
        left_ref, slot = lefts[left], slots[at]

        def one(step, _):
            cut = pl.ds(pl.multiple_of(step * tile, tile), tile)
            if turned:
                product = contract_last(left_ref[...], turned_buf[slot, cut, :])
            else:
                product = jnp.dot(
                    left_ref[...], plain_buf[slot, :, cut], preferred_element_type=jnp.float32
                )
            part[at, :, cut] = product.astype(jnp.bfloat16)
            return 0

        lax.fori_loop(0, span // tile, one, 0)

    def receive(stage, at):
        copies[stage, at].wait_recv()
        half = rows >> (stage + 1)
        step_rows = min(half, 16)
        held = current(stage, at)
        first = bits[stage] * half
        array, piece = chunks[at]

        def one(step, _):
            here = pl.ds(pl.multiple_of(step * step_rows, step_rows), step_rows)
            there = pl.ds(pl.multiple_of(first + step * step_rows, step_rows), step_rows)
            total = arrived[stage][at, here, :].astype(jnp.float32) + held[there, :].astype(
                jnp.float32
            )
            if stage == stages - 1:
                outs[array][here, pl.ds(piece * span, span)] = total
            else:
                arrived[stage][at, here, :] = total.astype(jnp.bfloat16)
            return 0

        lax.fori_loop(0, half // step_rows, one, 0)
        if stage < stages - 1:
            send(stage + 1, at)

    for turn in range(len(chunks) + stages):
        if turn < len(chunks):
            multiply(turn)
            send(0, turn)
        for stage in range(stages):
            at = turn - 1 - stage
            if 0 <= at < len(chunks):
                receive(stage, at)
    for copy in copies.values():
        copy.wait_send()


def reduce_mp(lefts, weights, plan, identity):
    count = lax.axis_size("mp")
    stages = count.bit_length() - 1
    rows, depth = lefts[0].shape
    width = weights[0].shape[0 if plan[0][1] else 1]
    amount = len(weights)
    per_array, span = column_chunks(width)
    chunks = amount * per_array
    turned_chunks = per_array * sum(turned for _, turned in plan)
    return pl.pallas_call(
        functools.partial(reduce_kernel, stages, plan, len(lefts)),
        out_shape=[jax.ShapeDtypeStruct((rows // count, width), jnp.float32)] * amount,
        in_specs=[pl.BlockSpec(memory_space=pltpu.VMEM)] * len(lefts)
        + [pl.BlockSpec(memory_space=pl.ANY)] * amount,
        out_specs=[pl.BlockSpec(memory_space=pltpu.VMEM)] * amount,
        scratch_shapes=[
            pltpu.VMEM((turned_chunks, span, depth), jnp.bfloat16),
            pltpu.VMEM((chunks - turned_chunks, depth, span), jnp.bfloat16),
            pltpu.VMEM((chunks, rows, span), jnp.bfloat16),
        ]
        + [
            pltpu.VMEM((chunks, rows >> (stage + 1), span), jnp.bfloat16)
            for stage in range(stages)
        ]
        + [
            pltpu.SemaphoreType.DMA((chunks,)),
            pltpu.SemaphoreType.DMA((stages, chunks)),
            pltpu.SemaphoreType.DMA((stages, chunks)),
        ],
        compiler_params=pltpu.CompilerParams(
            collective_id=identity, has_side_effects=True, vmem_limit_bytes=56 << 20
        ),
        cost_estimate=pl.CostEstimate(
            flops=2 * rows * depth * width * amount,
            bytes_accessed=amount * width * (depth + 20 * rows) * 2,
            transcendentals=0,
        ),
    )(*lefts, *weights)


def gather_kernel(stages, amount, *refs):
    shares, outs = refs[:amount], refs[amount : 2 * amount]
    send_sem, recv_sem = refs[2 * amount :]
    rows, width = outs[0].shape
    per_array, span = column_chunks(width)
    chunks = [(array, piece) for array in range(amount) for piece in range(per_array)]
    me = lax.axis_index("mp")
    bits, starts = halves_of(me, stages, rows)
    partners = [me + (1 - 2 * bits[stage]) * (1 << stage) for stage in range(stages)]
    least = rows >> stages
    own = pl.ds(pl.multiple_of(starts[stages], least), least)
    for array in range(amount):
        outs[array][own, :] = shares[array][...]
    greet(partners)

    copies = {}

    def send(stage, at):
        array, piece = chunks[at]
        size = rows >> (stage + 1)
        region = outs[array].at[
            pl.ds(pl.multiple_of(starts[stage + 1], size), size), pl.ds(piece * span, span)
        ]
        copies[stage, at] = pltpu.make_async_remote_copy(
            src_ref=region,
            dst_ref=region,
            send_sem=send_sem.at[stage, at],
            recv_sem=recv_sem.at[stage, at],
            device_id={"mp": partners[stage]},
            device_id_type=pl.DeviceIdType.MESH,
        )
        copies[stage, at].start()

    for turn in range(len(chunks) + stages):
        if turn < len(chunks):
            send(stages - 1, turn)
        for step in range(stages):
            at = turn - 1 - step
            stage = stages - 1 - step
            if 0 <= at < len(chunks):
                copies[stage, at].wait_recv()
                if stage > 0:
                    send(stage - 1, at)
    for copy in copies.values():
        copy.wait_send()


def gather_mp(shares, identity):
    count = lax.axis_size("mp")
    stages = count.bit_length() - 1
    rows, width = shares[0].shape
    amount = len(shares)
    chunks = amount * column_chunks(width)[0]
    return pl.pallas_call(
        functools.partial(gather_kernel, stages, amount),
        out_shape=[jax.ShapeDtypeStruct((rows * count, width), jnp.bfloat16)] * amount,
        in_specs=[pl.BlockSpec(memory_space=pltpu.VMEM)] * amount,
        out_specs=[pl.BlockSpec(memory_space=pltpu.VMEM)] * amount,
        scratch_shapes=[
            pltpu.SemaphoreType.DMA((stages, chunks)),
            pltpu.SemaphoreType.DMA((stages, chunks)),
        ],
        compiler_params=pltpu.CompilerParams(
            collective_id=identity, has_side_effects=True, vmem_limit_bytes=48 << 20
        ),
        cost_estimate=pl.CostEstimate(
            flops=0, bytes_accessed=amount * width * rows * count * 40, transcendentals=0
        ),
    )(*shares)


def per_device(tokens, gate_weight, up_weight, down_weight, factor_self, factor_cross, cotangent):
    tok_rows, local_width = tokens.shape
    per_dev = local_width // BLOCK
    local_bits = per_dev.bit_length() - 1
    output_grad = gather_dp(cotangent)
    current = tokens.reshape(tok_rows, per_dev, BLOCK)
    kept = []
    for degree in range(SECTIONS):
        self_mat = factor_self[degree].reshape(per_dev, BLOCK, BLOCK)
        cross_mat = factor_cross[degree].reshape(per_dev, BLOCK, BLOCK)
        if degree < local_bits:
            partner = local_partner(current, degree)
            kept += [current.reshape(tok_rows, local_width)]
        else:
            partner = swapped(current, "mp", degree - local_bits)
            kept += [current.reshape(tok_rows, local_width), partner.reshape(tok_rows, local_width)]
        result = jnp.einsum("tkb,kbc->tkc", current, self_mat, preferred_element_type=jnp.float32)
        result = result + jnp.einsum(
            "tkb,kbc->tkc", partner, cross_mat, preferred_element_type=jnp.float32
        )
        current = result.astype(jnp.bfloat16)
    rotated = current.reshape(tok_rows, local_width)
    segment = gather_dp(rotated)
    kept = gather_dp(jnp.concatenate(kept, axis=1))
    hidden_grad, gate_sum, up_sum = reduce_mp(
        [output_grad, segment],
        [down_weight, gate_weight, up_weight],
        ((0, True), (1, False), (1, False)),
        0,
    )
    logistic = jax.nn.sigmoid(gate_sum)
    gate_grad = (hidden_grad * up_sum * logistic * (1.0 + gate_sum * (1.0 - logistic))).astype(
        jnp.bfloat16
    )
    up_grad = (hidden_grad * gate_sum * logistic).astype(jnp.bfloat16)
    hidden = (jax.nn.silu(gate_sum) * up_sum).astype(jnp.bfloat16)
    gate_all, up_all, hidden_all = gather_mp([gate_grad, up_grad, hidden], 1)
    rot_terms = contract_last(gate_all, gate_weight) + contract_last(up_all, up_weight)
    gradient = scatter_dp(rot_terms)
    partial_value = jnp.dot(hidden_all, down_weight, preferred_element_type=jnp.float32)
    mixed_out = scatter_dp(partial_value)

    all_rows = kept.shape[0]
    kept = kept.reshape(all_rows, -1, per_dev, BLOCK)
    place = kept.shape[1]
    gradient = gradient.reshape(tok_rows, per_dev, BLOCK)
    self_list = [None] * SECTIONS
    cross_list = [None] * SECTIONS
    for degree in reversed(range(SECTIONS)):
        self_mat = factor_self[degree].reshape(per_dev, BLOCK, BLOCK)
        cross_mat = factor_cross[degree].reshape(per_dev, BLOCK, BLOCK)
        gathered = gather_dp(gradient)
        if degree < local_bits:
            place -= 1
            ours = kept[:, place]
            theirs = local_partner(ours, degree)
        else:
            place -= 2
            ours, theirs = kept[:, place], kept[:, place + 1]
        self_list[degree] = jnp.einsum(
            "tkb,tkc->kbc", ours, gathered, preferred_element_type=jnp.float32
        ).reshape(per_dev * BLOCK, BLOCK)
        cross_list[degree] = jnp.einsum(
            "tkb,tkc->kbc", theirs, gathered, preferred_element_type=jnp.float32
        ).reshape(per_dev * BLOCK, BLOCK)
        direct = jnp.einsum("tkc,kbc->tkb", gradient, self_mat, preferred_element_type=jnp.float32)
        carried = jnp.einsum(
            "tkc,kbc->tkb", gradient, cross_mat, preferred_element_type=jnp.float32
        )
        if degree < local_bits:
            returned = local_partner(carried, degree)
        else:
            returned = swapped(carried.astype(jnp.bfloat16), "mp", degree - local_bits).astype(
                carried.dtype
            )
        gradient = (direct + returned).astype(jnp.bfloat16)
    self_grad = jnp.stack(self_list)
    cross_grad = jnp.stack(cross_list)
    return (mixed_out, gradient.reshape(tok_rows, local_width), self_grad, cross_grad)


def solution(mesh):
    return jax.shard_map(
        per_device,
        mesh=mesh,
        in_specs=(
            P("dp", "mp"),
            P("mp", "dp"),
            P("mp", "dp"),
            P("dp", "mp"),
            P(None, "mp", None),
            P(None, "mp", None),
            P("dp", "mp"),
        ),
        out_specs=(P("dp", "mp"), P("dp", "mp"), P(None, "mp", None), P(None, "mp", None)),
        check_vma=False,
    )
```
